32 devices in a mesh: parts: 2 (over y), blk: 8 (over z, x), layer: 2 (over core).
Axes of the slice: x: 2, y: 2, z: 4, core: 2. Of those that a mesh axis runs over, the one named last changes fastest.
Arguments:
- query_grads: bfloat16 [2, 128, 2048], P('layer', ('parts', 'blk')), parts along dimension 1, may hold values from -0.09375 to 0.09375
- train_grads: bfloat16 [2, 12288, 2048], P('layer', ('parts', 'blk')), parts along dimension 1, may hold values from -6 to 6
- fisher: bfloat16 [2, 2048, 2048], P('layer', 'blk'), as said below
Outputs:
- scores: bfloat16 [64, 12288], P(None, ('parts', 'blk', 'layer')), parts along dimension 1
The draws below stay inside these ranges and needn't reach their ends.
There are 2 independent parts, one for each index of `parts`. The reference program is written for one: setup_inputs(seed, part) draws one part's arguments, and reference() takes and returns one part's arrays. A program takes and returns all parts, laid end to end along the dimension named above; an argument that names none is the same for every part. Nothing has to cross between parts.
Inputs may be any that keep to these rules, and one draw needn't show every extreme that they name: `fisher`: each layer's block is symmetric.
All inputs are finite; a program needn't handle non-finite values.
Results may differ from the reference program's by a relative error of at most 0.005.
Values may be sent and summed in bfloat16 or wider, within the bound.
A program may use at most 64 MiB of HBM per device.

```python
import math
import jax
import jax.numpy as jnp

K = 2048
LAYERS = 2
Q_TOTAL = 64
T_TOTAL = 6144


def draw_fisher(key, part):
    key = jax.random.fold_in(key, 7)
    first_key, second_key = jax.random.split(key)
    raw = jax.random.normal(first_key, (LAYERS, K, K), jnp.float32)
    diagonal = jax.random.uniform(second_key, (LAYERS, K), jnp.float32, 0.8, 1.6)
    symmetric = (raw + jnp.swapaxes(raw, 1, 2)) * (0.4 / math.sqrt(2.0 * K))
    identity = jnp.eye(K, dtype=jnp.float32)
    return (symmetric + identity[None, :, :] * diagonal[:, :, None]).astype(jnp.bfloat16)


def shard_levels(own_key, shape, cuts, least, top_value):
    def one(axis_at, blocks):
        heights = jax.random.uniform(jax.random.fold_in(jax.random.fold_in(own_key, 6), axis_at), (blocks,), jnp.float32, least / len(cuts), top_value / len(cuts))
        return jnp.repeat(jnp.exp(heights), shape[axis_at] // blocks).reshape((-1,) + (1,) * (len(shape) - axis_at - 1))

    loudness = one(*cuts[0])
    for cut in cuts[1:]:
        loudness = loudness * one(*cut)
    return loudness


def centred(stream_key, shape, width, limit, cuts=(), held_as=jnp.bfloat16):
    level = shard_levels(stream_key, shape, cuts, -0.22, 0.18) if cuts else 1.0
    values = jax.random.normal(stream_key, shape, jnp.float32) * width * level
    return jnp.minimum(jnp.maximum(values, -limit), limit).astype(held_as)


def setup_inputs(seed: int = 0, part: int = 0) -> dict:
    seeds = jax.random.split(jax.random.key(seed), 4)
    own_keys = jax.random.split(jax.random.fold_in(seeds[3], part), 4)
    query_grads = centred(own_keys[0], (LAYERS, Q_TOTAL, K), (2 * K) ** -0.5, 0.09375, ((0, 2), (1, 8)))
    train_grads = centred(own_keys[1], (LAYERS, T_TOTAL, K), 1.0, 6.0, ((0, 2), (1, 8)))
    fisher = draw_fisher(jax.random.fold_in(seeds[3], 71), part)
    return dict(query_grads=query_grads, train_grads=train_grads, fisher=fisher)


def reference(query_grads, train_grads, fisher):
    accumulated = jnp.zeros((Q_TOTAL, T_TOTAL), jnp.float32)
    for layer_index in range(LAYERS):
        prepared = jnp.dot(query_grads[layer_index], fisher[layer_index], preferred_element_type=jnp.float32).astype(jnp.bfloat16)
        accumulated = accumulated + jnp.dot(prepared, train_grads[layer_index].T, preferred_element_type=jnp.float32)
    return accumulated.astype(jnp.bfloat16)
```

```python
import functools

import jax
import jax.numpy as jnp
from jax import lax
from jax.experimental import pallas as pl
from jax.experimental.pallas import tpu as pltpu
from jax.sharding import PartitionSpec as P

MESH = pl.DeviceIdType.MESH
CONTRACT = (((1,), (1,)), ((), ()))


def dot_t(a, b):
    return lax.dot_general(a, b, CONTRACT, preferred_element_type=jnp.float32)


def kernel(n, q_ref, t_ref, f_ref, out_ref, q_all, t_all, f_all, p_all, part, other,
           q_send, q_recv, p_send, p_recv, s_send, s_recv, in_sem):
    me = lax.axis_index("blk")
    layer = lax.axis_index("layer")
    half = t_all.shape[1]
    width = f_all.shape[0]

    load_q = pltpu.make_async_copy(q_ref.at[0], q_all.at[me], in_sem.at[0])
    load_f = pltpu.make_async_copy(f_ref.at[0], f_all, in_sem.at[1])
    load_t = [
        pltpu.make_async_copy(
            t_ref.at[0, pl.ds(pl.multiple_of(start * half, half), half), :], t_all.at[slot], in_sem.at[2 + slot]
        )
        for slot, start in ((0, 1 - layer), (1, layer))
    ]
    load_q.start()
    load_f.start()
    load_t[0].start()
    load_t[1].start()

    barrier = pltpu.get_barrier_semaphore()
    for step in range(1, n):
        pl.semaphore_signal(barrier, inc=1, device_id={"blk": lax.rem(me + step, n)}, device_id_type=MESH)
    pl.semaphore_signal(barrier, inc=1, device_id={"layer": 1 - layer}, device_id_type=MESH)
    load_q.wait()
    pl.semaphore_wait(barrier, n)

    def push(buf, step, send, recv):
        return pltpu.make_async_remote_copy(
            src_ref=buf.at[me], dst_ref=buf.at[me], send_sem=send.at[step], recv_sem=recv.at[step],
            device_id={"blk": lax.rem(me + step, n)}, device_id_type=MESH,
        )

    def arrival(buf, step, send, recv):
        source = lax.rem(me + n - step, n)
        return pltpu.make_async_remote_copy(
            src_ref=buf.at[source], dst_ref=buf.at[source], send_sem=send.at[step], recv_sem=recv.at[step],
            device_id={"blk": lax.rem(me + step, n)}, device_id_type=MESH,
        )

    for step in range(1, n):
        push(q_all, step, q_send, q_recv).start()
    load_f.wait()
    for step in range(1, n):
        arrival(q_all, step, q_send, q_recv).wait_recv()
    queries = q_all[...].reshape(-1, q_all.shape[2])
    p_all[me] = dot_t(queries, f_all[...]).astype(jnp.bfloat16)
    for step in range(1, n):
        push(p_all, step, p_send, p_recv).start()
    load_t[0].wait()
    load_t[1].wait()

    def term(source):
        columns = pl.ds(pl.multiple_of(source * width, width), width)
        block = p_all[source]
        for slot in range(2):
            yield dot_t(block, t_all[slot, :, columns])

    total = list(term(me))
    for step in range(1, n):
        arrival(p_all, step, p_send, p_recv).wait_recv()
        total = [a + b for a, b in zip(total, term(lax.rem(me + n - step, n)))]
    part[...] = total[0]
    swap = pltpu.make_async_remote_copy(
        src_ref=part, dst_ref=other, send_sem=s_send, recv_sem=s_recv,
        device_id={"layer": 1 - layer}, device_id_type=MESH,
    )
    swap.start()
    for step in range(1, n):
        push(q_all, step, q_send, q_recv).wait_send()
        push(p_all, step, p_send, p_recv).wait_send()
    swap.wait()
    out_ref[...] = (total[1] + other[...]).astype(out_ref.dtype)


def fused(n, queries, training, fisher):
    rows = queries.shape[1] * n
    k = queries.shape[2]
    half = training.shape[1] // 2
    width = fisher.shape[1]
    vmem = pltpu.VMEM
    dma = pltpu.SemaphoreType.DMA
    return pl.pallas_call(
        functools.partial(kernel, n),
        out_shape=jax.ShapeDtypeStruct((rows, half), jnp.bfloat16),
        in_specs=[pl.BlockSpec(memory_space=pltpu.HBM)] * 3,
        out_specs=pl.BlockSpec(memory_space=vmem),
        scratch_shapes=[
            vmem((n, queries.shape[1], k), jnp.bfloat16),
            vmem((2, half, k), jnp.bfloat16),
            vmem((width, k), jnp.bfloat16),
            vmem((n, rows, width), jnp.bfloat16),
            vmem((rows, half), jnp.float32),
            vmem((rows, half), jnp.float32),
            dma((n,)), dma((n,)), dma((n,)), dma((n,)), dma, dma, dma((4,)),
        ],
        compiler_params=pltpu.CompilerParams(
            collective_id=0, has_side_effects=True, vmem_limit_bytes=48 * 1024 * 1024
        ),
    )(queries, training, fisher)


def plain(queries, training, fisher):
    gathered = lax.all_gather(queries[0], "blk", axis=0, tiled=True)
    prepared_columns = dot_t(gathered, fisher[0]).astype(jnp.bfloat16)
    prepared = lax.all_gather(prepared_columns, "blk", axis=1, tiled=True)
    partial_scores = dot_t(prepared, training[0])
    summed = lax.psum_scatter(partial_scores, "layer", scatter_dimension=1, tiled=True)
    return summed.astype(jnp.bfloat16)


def solution(mesh):
    n = mesh.shape["blk"]

    def local(queries, training, fisher):
        if n > 16 or fisher.shape[1] % 128:
            return plain(queries, training, fisher)
        return fused(n, queries, training, fisher)

    return jax.shard_map(
        local,
        mesh=mesh,
        in_specs=(
            P("layer", ("parts", "blk"), None),
            P("layer", ("parts", "blk"), None),
            P("layer", "blk", None),
        ),
        out_specs=P(None, ("parts", "blk", "layer")),
        check_vma=False,
    )
```

```python
import functools

import jax
import jax.numpy as jnp
from jax import lax
from jax.experimental import pallas as pl
from jax.experimental.pallas import tpu as pltpu
from jax.sharding import PartitionSpec as P

MESH = pl.DeviceIdType.MESH
CONTRACT = (((1,), (1,)), ((), ()))


def dot_t(a, b):
    return lax.dot_general(a, b, CONTRACT, preferred_element_type=jnp.float32)


def kernel(n, q_ref, t_ref, f_ref, out_ref, q_all, t_all, f_all, p_all, part, mine, other,
           q_send, q_recv, p_send, p_recv, s_send, s_recv, in_sem):
    me = lax.axis_index("blk")
    layer = lax.axis_index("layer")
    half = t_all.shape[1]
    width = f_all.shape[0]

    load_q = pltpu.make_async_copy(q_ref.at[0], q_all.at[me], in_sem.at[0])
    load_f = pltpu.make_async_copy(f_ref.at[0], f_all, in_sem.at[1])
    load_t = [
        pltpu.make_async_copy(
            t_ref.at[0, pl.ds(pl.multiple_of(start * half, half), half), :], t_all.at[slot], in_sem.at[2 + slot]
        )
        for slot, start in ((0, 1 - layer), (1, layer))
    ]
    load_q.start()
    load_f.start()
    load_t[0].start()
    load_t[1].start()

    targets = [lax.rem(me + i, n) for i in range(n)]
    sources = [lax.rem(me + n - i, n) for i in range(n)]
    cut = n // 2 - 1
    early, late = range(n - 1, cut, -1), range(cut, 0, -1)

    barrier = pltpu.get_barrier_semaphore()
    for i in range(1, n):
        pl.semaphore_signal(barrier, inc=1, device_id={"blk": targets[i]}, device_id_type=MESH)
    pl.semaphore_signal(barrier, inc=1, device_id={"layer": 1 - layer}, device_id_type=MESH)
    load_q.wait()
    pl.semaphore_wait(barrier, n)

    def push(buf, at, i, send, recv):
        return pltpu.make_async_remote_copy(
            src_ref=buf.at[at], dst_ref=buf.at[at], send_sem=send.at[i], recv_sem=recv.at[i],
            device_id={"blk": targets[i]}, device_id_type=MESH,
        )

    for i in range(1, n):
        push(q_all, me, i, q_send, q_recv).start()
    load_f.wait()
    for i in range(1, n):
        push(q_all, sources[i], i, q_send, q_recv).wait_recv()
    queries = q_all[...].reshape(-1, q_all.shape[2])
    p_all[me] = dot_t(queries, f_all[...]).astype(jnp.bfloat16)
    for i in range(1, n):
        push(p_all, me, i, p_send, p_recv).start()
    load_t[0].wait()
    load_t[1].wait()

    def term(source, slot):
        columns = pl.ds(pl.multiple_of(source * width, width), width)
        return dot_t(p_all[source], t_all[slot, :, columns])

    total = [term(me, 0), term(me, 1)]
    for i in early:
        push(p_all, sources[i], i, p_send, p_recv).wait_recv()
        total = [total[slot] + term(sources[i], slot) for slot in range(2)]
    mine[...] = total[1]
    total = total[0]
    for i in late:
        push(p_all, sources[i], i, p_send, p_recv).wait_recv()
        total = total + term(sources[i], 0)
    part[...] = total
    swap = pltpu.make_async_remote_copy(
        src_ref=part, dst_ref=other, send_sem=s_send, recv_sem=s_recv,
        device_id={"layer": 1 - layer}, device_id_type=MESH,
    )
    swap.start()
    total = mine[...]
    for i in late:
        total = total + term(sources[i], 1)
    for i in range(1, n):
        push(q_all, me, i, q_send, q_recv).wait_send()
        push(p_all, me, i, p_send, p_recv).wait_send()
    swap.wait()
    out_ref[...] = (total + other[...]).astype(out_ref.dtype)


def fused(n, queries, training, fisher):
    rows = queries.shape[1] * n
    k = queries.shape[2]
    half = training.shape[1] // 2
    width = fisher.shape[1]
    vmem = pltpu.VMEM
    dma = pltpu.SemaphoreType.DMA
    return pl.pallas_call(
        functools.partial(kernel, n),
        out_shape=jax.ShapeDtypeStruct((rows, half), jnp.bfloat16),
        in_specs=[pl.BlockSpec(memory_space=pltpu.HBM)] * 3,
        out_specs=pl.BlockSpec(memory_space=vmem),
        scratch_shapes=[
            vmem((n, queries.shape[1], k), jnp.bfloat16),
            vmem((2, half, k), jnp.bfloat16),
            vmem((width, k), jnp.bfloat16),
            vmem((n, rows, width), jnp.bfloat16),
            vmem((rows, half), jnp.float32),
            vmem((rows, half), jnp.float32),
            vmem((rows, half), jnp.float32),
            dma((n,)), dma((n,)), dma((n,)), dma((n,)), dma, dma, dma((4,)),
        ],
        compiler_params=pltpu.CompilerParams(
            collective_id=0, has_side_effects=True, vmem_limit_bytes=63 * 1024 * 1024
        ),
    )(queries, training, fisher)


def plain(queries, training, fisher):
    gathered = lax.all_gather(queries[0], "blk", axis=0, tiled=True)
    prepared_columns = dot_t(gathered, fisher[0]).astype(jnp.bfloat16)
    prepared = lax.all_gather(prepared_columns, "blk", axis=1, tiled=True)
    partial_scores = dot_t(prepared, training[0])
    summed = lax.psum_scatter(partial_scores, "layer", scatter_dimension=1, tiled=True)
    return summed.astype(jnp.bfloat16)


def solution(mesh):
    n = mesh.shape["blk"]

    def local(queries, training, fisher):
        if n > 16 or n % 2 or fisher.shape[1] % 128:
            return plain(queries, training, fisher)
        return fused(n, queries, training, fisher)

    return jax.shard_map(
        local,
        mesh=mesh,
        in_specs=(
            P("layer", ("parts", "blk"), None),
            P("layer", ("parts", "blk"), None),
            P("layer", "blk", None),
        ),
        out_specs=P(None, ("parts", "blk", "layer")),
        check_vma=False,
    )
```

```python
import functools

import jax
import jax.numpy as jnp
from jax import lax
from jax.experimental import pallas as pl
from jax.experimental.pallas import tpu as pltpu
from jax.sharding import PartitionSpec as P

MESH = pl.DeviceIdType.MESH
CONTRACT = (((1,), (1,)), ((), ()))


def dot_t(a, b):
    return lax.dot_general(a, b, CONTRACT, preferred_element_type=jnp.float32)


def kernel(n, q_ref, t_ref, f_ref, out_ref, q_all, t_all, f_all, p_all, part, mine, other,
           q_send, q_recv, p_send, p_recv, s_send, s_recv, in_sem):
    me = lax.axis_index("blk")
    layer = lax.axis_index("layer")
    half = t_all.shape[1]
    width = f_all.shape[0]

    load_q = pltpu.make_async_copy(q_ref.at[0], q_all.at[me], in_sem.at[0])
    load_f = pltpu.make_async_copy(f_ref.at[0], f_all, in_sem.at[1])
    load_t = [
        pltpu.make_async_copy(
            t_ref.at[0, pl.ds(pl.multiple_of(start * half, half), half), :], t_all.at[slot], in_sem.at[2 + slot]
        )
        for slot, start in ((0, 1 - layer), (1, layer))
    ]
    load_q.start()
    load_f.start()
    load_t[0].start()
    load_t[1].start()

    targets = [lax.rem(me + i, n) for i in range(n)]
    sources = [lax.rem(me + n - i, n) for i in range(n)]
    cut = n // 2 - 1
    early, late = range(n - 1, cut, -1), range(cut, 0, -1)

    barrier = pltpu.get_barrier_semaphore()
    for i in range(1, n):
        pl.semaphore_signal(barrier, inc=1, device_id={"blk": targets[i]}, device_id_type=MESH)
    pl.semaphore_signal(barrier, inc=1, device_id={"layer": 1 - layer}, device_id_type=MESH)
    load_q.wait()
    pl.semaphore_wait(barrier, n)

    def push(buf, at, i, send, recv):
        return pltpu.make_async_remote_copy(
            src_ref=buf.at[at], dst_ref=buf.at[at], send_sem=send.at[i], recv_sem=recv.at[i],
            device_id={"blk": targets[i]}, device_id_type=MESH,
        )

    for i in [*range(n - 1, 0, -2), *range(n - 2, 0, -2)]:
        push(q_all, me, i, q_send, q_recv).start()
    load_f.wait()
    for i in range(1, n):
        push(q_all, sources[i], i, q_send, q_recv).wait_recv()
    queries = q_all[...].reshape(-1, q_all.shape[2])
    p_all[me] = dot_t(queries, f_all[...]).astype(jnp.bfloat16)
    for i in range(1, n):
        push(p_all, me, i, p_send, p_recv).start()
    load_t[0].wait()
    load_t[1].wait()

    def term(source, slot):
        columns = pl.ds(pl.multiple_of(source * width, width), width)
        return dot_t(p_all[source], t_all[slot, :, columns])

    total = [term(me, 0), term(me, 1)]
    for i in early:
        push(p_all, sources[i], i, p_send, p_recv).wait_recv()
        total = [total[slot] + term(sources[i], slot) for slot in range(2)]
    mine[...] = total[1]
    total = total[0]
    for i in late:
        push(p_all, sources[i], i, p_send, p_recv).wait_recv()
        total = total + term(sources[i], 0)
    part[...] = total
    swap = pltpu.make_async_remote_copy(
        src_ref=part, dst_ref=other, send_sem=s_send, recv_sem=s_recv,
        device_id={"layer": 1 - layer}, device_id_type=MESH,
    )
    swap.start()
    total = mine[...]
    for i in late:
        total = total + term(sources[i], 1)
    for i in range(1, n):
        push(q_all, me, i, q_send, q_recv).wait_send()
        push(p_all, me, i, p_send, p_recv).wait_send()
    swap.wait()
    out_ref[...] = (total + other[...]).astype(out_ref.dtype)


def fused(n, queries, training, fisher):
    rows = queries.shape[1] * n
    k = queries.shape[2]
    half = training.shape[1] // 2
    width = fisher.shape[1]
    vmem = pltpu.VMEM
    dma = pltpu.SemaphoreType.DMA
    return pl.pallas_call(
        functools.partial(kernel, n),
        out_shape=jax.ShapeDtypeStruct((rows, half), jnp.bfloat16),
        in_specs=[pl.BlockSpec(memory_space=pltpu.HBM)] * 3,
        out_specs=pl.BlockSpec(memory_space=vmem),
        scratch_shapes=[
            vmem((n, queries.shape[1], k), jnp.bfloat16),
            vmem((2, half, k), jnp.bfloat16),
            vmem((width, k), jnp.bfloat16),
            vmem((n, rows, width), jnp.bfloat16),
            vmem((rows, half), jnp.float32),
            vmem((rows, half), jnp.float32),
            vmem((rows, half), jnp.float32),
            dma((n,)), dma((n,)), dma((n,)), dma((n,)), dma, dma, dma((4,)),
        ],
        compiler_params=pltpu.CompilerParams(
            collective_id=0, has_side_effects=True, vmem_limit_bytes=63 * 1024 * 1024
        ),
    )(queries, training, fisher)


def plain(queries, training, fisher):
    gathered = lax.all_gather(queries[0], "blk", axis=0, tiled=True)
    prepared_columns = dot_t(gathered, fisher[0]).astype(jnp.bfloat16)
    prepared = lax.all_gather(prepared_columns, "blk", axis=1, tiled=True)
    partial_scores = dot_t(prepared, training[0])
    summed = lax.psum_scatter(partial_scores, "layer", scatter_dimension=1, tiled=True)
    return summed.astype(jnp.bfloat16)


def solution(mesh):
    n = mesh.shape["blk"]

    def local(queries, training, fisher):
        if n > 16 or n % 2 or fisher.shape[1] % 128:
            return plain(queries, training, fisher)
        return fused(n, queries, training, fisher)

    return jax.shard_map(
        local,
        mesh=mesh,
        in_specs=(
            P("layer", ("parts", "blk"), None),
            P("layer", ("parts", "blk"), None),
            P("layer", "blk", None),
        ),
        out_specs=P(None, ("parts", "blk", "layer")),
        check_vma=False,
    )
```
